512 devices in a mesh: slab: 32 (over z, core), orb: 16 (over y, x).
Axes of the slice: x: 4, y: 4, z: 16, core: 2. Of those that a mesh axis runs over, the one named last changes fastest.
Arguments:
- diag_even: float32 [64, 2, 512, 512], P('slab', None, 'orb'), may hold values from -1.3 to 10
- odd_green: float32 [64, 2, 512, 512], P('slab', None, 'orb'), may hold values from -0.3 to 0.45
- lower: float32 [128, 2, 512, 512], P('slab', None, 'orb'), may hold values from -1.8 to 1.8
- upper: float32 [128, 2, 512, 512], P('slab', None, 'orb'), may hold values from -1.8 to 1.8
Outputs:
- final_diag: float32 [32, 2, 512, 512], P('slab', None, 'orb')
- final_lower: float32 [32, 2, 512, 512], P('slab', None, 'orb')
- final_upper: float32 [32, 2, 512, 512], P('slab', None, 'orb')
The draws below stay inside these ranges and needn't reach their ends.
All inputs are finite; a program needn't handle non-finite values.
Results may differ from the reference program's by a relative error of at most 0.00012.
Values sent between devices are 32-bit elements; how exact they have to be, the bound alone decides.
No kernel may reach another device: no remote copies, remote signals or barrier semaphores. Data moves between devices by JAX's collectives and lax.ppermute only.
A program may use at most 64 MiB of HBM per device.

```python
import math
import jax
import jax.numpy as jnp
from jax import lax

M = 512
NS = 128


def with_diagonal(key, off_re, off_im, count):
    radius = jax.random.uniform(jax.random.fold_in(key, 1), (count, M), jnp.float32, 1.0, 1.8)
    phase = jax.random.uniform(jax.random.fold_in(key, 2), (count, M), jnp.float32, -math.pi, math.pi)
    identity = jnp.eye(M, dtype=bool)
    real_part = jnp.where(identity, (radius * jnp.cos(phase))[:, :, None], off_re)
    imag_part = jnp.where(identity, (radius * jnp.sin(phase))[:, :, None], off_im)
    return jnp.stack([real_part, imag_part], axis=1)


def draw_diag_even(key, part):
    key = jax.random.fold_in(key, 11)
    subkeys = jax.random.split(key, 4)
    extent = (NS // 2, M, M)
    spread = 1.7 / math.sqrt(M)
    raw_re = spread * jax.random.truncated_normal(subkeys[0], -4.0, 4.0, extent, jnp.float32)
    raw_im = spread * jax.random.truncated_normal(subkeys[1], -4.0, 4.0, extent, jnp.float32)
    row_index = jnp.arange(M)[:, None]
    col_index = jnp.arange(M)[None, :]
    above = row_index < col_index
    off_re = jnp.where(above, raw_re, jnp.swapaxes(raw_re, 1, 2))
    off_im = jnp.where(above, raw_im, -jnp.swapaxes(raw_im, 1, 2))
    diag_re = jax.random.uniform(subkeys[2], (NS // 2, M), jnp.float32, 6.0, 10.0)
    diag_im = jax.random.uniform(subkeys[3], (NS // 2, M), jnp.float32, 0.2, 1.0)
    identity = row_index == col_index
    real_part = jnp.where(identity, diag_re[:, :, None], off_re)
    imag_part = jnp.where(identity, diag_im[:, :, None], off_im)
    return jnp.stack([real_part, imag_part], axis=1)


def draw_odd_green(key, part):
    key = jax.random.fold_in(key, 23)
    subkeys = jax.random.split(key, 3)
    extent = (NS // 2, 2, M, M)
    spread = 0.07 / math.sqrt(M)
    coupling = spread * jax.random.truncated_normal(subkeys[0], -4.0, 4.0, extent, jnp.float32)
    diag_re = jax.random.uniform(subkeys[1], (NS // 2, M), jnp.float32, 0.15, 0.4)
    diag_im = jax.random.uniform(subkeys[2], (NS // 2, M), jnp.float32, -0.25, -0.02)
    identity = jnp.eye(M, dtype=bool)
    real_part = jnp.where(identity, diag_re[:, :, None], coupling[:, 0])
    imag_part = jnp.where(identity, diag_im[:, :, None], coupling[:, 1])
    return jnp.stack([real_part, imag_part], axis=1)


def draw_lower(key, part):
    key = jax.random.fold_in(key, 37)
    extent = (NS, 2, M, M)
    spread = 0.45 / math.sqrt(M)
    coupling = spread * jax.random.truncated_normal(jax.random.fold_in(key, 5), -4.0, 4.0, extent, jnp.float32)
    return with_diagonal(key, coupling[:, 0], coupling[:, 1], NS)


def draw_upper(key, part):
    key = jax.random.fold_in(key, 53)
    extent = (NS, 2, M, M)
    spread = 0.45 / math.sqrt(M)
    coupling = spread * jax.random.truncated_normal(jax.random.fold_in(key, 5), -4.0, 4.0, extent, jnp.float32)
    return with_diagonal(key, coupling[:, 0], coupling[:, 1], NS)


def setup_inputs(seed: int = 0) -> dict:
    key_of = jax.random.split(jax.random.key(seed), 5)
    return {
        "diag_even": draw_diag_even(jax.random.fold_in(key_of[4], 71), 0),
        "odd_green": draw_odd_green(jax.random.fold_in(key_of[4], 71), 0),
        "lower": draw_lower(jax.random.fold_in(key_of[4], 71), 0),
        "upper": draw_upper(jax.random.fold_in(key_of[4], 71), 0),
    }


def matmul_high(first, second):
    return jnp.matmul(first, second, precision=lax.Precision.HIGHEST)


def complex_product(first, second):
    first_re = first[..., 0, :, :]
    first_im = first[..., 1, :, :]
    second_re = second[..., 0, :, :]
    second_im = second[..., 1, :, :]
    real_part = matmul_high(first_re, second_re) - matmul_high(first_im, second_im)
    imag_part = matmul_high(first_re, second_im) + matmul_high(first_im, second_re)
    return jnp.stack([real_part, imag_part], axis=-3)


def eliminate(group):
    inverse, coupling_up, coupling_down = group
    return complex_product(inverse, coupling_up), complex_product(inverse, coupling_down)


def combine_kept(group):
    diag_block, lower_block, upper_block, left_up, left_down, right_up, right_down = group
    new_diag = diag_block - complex_product(lower_block, left_up) - complex_product(upper_block, right_down)
    return new_diag, -complex_product(lower_block, left_down), -complex_product(upper_block, right_up)


def newton_inverse(block):
    size_m = block.shape[-1]
    diag_re = jnp.diagonal(block[0])
    diag_im = jnp.diagonal(block[1])
    modulus = diag_re * diag_re + diag_im * diag_im
    weight_re = diag_re / modulus
    weight_im = -diag_im / modulus
    inner_re = weight_re[:, None] * block[0] - weight_im[:, None] * block[1]
    inner_im = weight_re[:, None] * block[1] + weight_im[:, None] * block[0]
    outer_re = inner_re * weight_re[None, :] - inner_im * weight_im[None, :]
    outer_im = inner_re * weight_im[None, :] + inner_im * weight_re[None, :]
    identity = jnp.eye(size_m, dtype=block.dtype)
    first = jnp.stack([2.0 * identity * weight_re[:, None] - outer_re, 2.0 * identity * weight_im[:, None] - outer_im])
    return 2.0 * first - complex_product(first, complex_product(block, first))


def reference(diag_even, odd_green, lower, upper):
    up_odd, down_odd = lax.map(eliminate, (odd_green, upper[1::2], lower[1::2]))
    new_diag, new_lower, new_upper = lax.map(combine_kept, (diag_even, lower[0::2], upper[0::2], jnp.roll(up_odd, 1, 0), jnp.roll(down_odd, 1, 0), up_odd, down_odd))
    inverse_two = lax.map(newton_inverse, new_diag[1::2])
    up_two, down_two = lax.map(eliminate, (inverse_two, new_upper[1::2], new_lower[1::2]))
    final_diag, final_lower, final_upper = lax.map(combine_kept, (new_diag[0::2], new_lower[0::2], new_upper[0::2], jnp.roll(up_two, 1, 0), jnp.roll(down_two, 1, 0), up_two, down_two))
    return final_diag, final_lower, final_upper
```

```python
import jax
import jax.numpy as jnp
from jax import lax
from jax.sharding import PartitionSpec as P

SIDE = 4


def shifted(value, axis, steps):
    count = lax.axis_size(axis)
    pairs = [(source, (source + steps) % count) for source in range(count)]
    return lax.ppermute(value, axis, pairs)


def orb_shift(value, dy, dx):
    pairs = []
    for y in range(SIDE):
        for x in range(SIDE):
            pairs.append((y * SIDE + x, ((y + dy) % SIDE) * SIDE + (x + dx) % SIDE))
    return lax.ppermute(value, "orb", pairs)


def gathered_by_permutes(value):
    index = lax.axis_index("orb")
    place_y = index // SIDE
    place_x = index % SIDE
    along_x = [value] + [orb_shift(value, 0, step) for step in range(1, SIDE)]
    line = jnp.stack(along_x[::-1] + along_x[::-1])
    line = lax.dynamic_slice_in_dim(line, SIDE - 1 - place_x, SIDE, 0)
    along_y = [line] + [orb_shift(line, step, 0) for step in range(1, SIDE)]
    plane = jnp.stack(along_y[::-1] + along_y[::-1])
    plane = lax.dynamic_slice_in_dim(plane, SIDE - 1 - place_y, SIDE, 0)
    return plane.reshape(SIDE * SIDE * value.shape[0], value.shape[1])


def packed(block):
    return jnp.concatenate([block[..., 0, :, :], block[..., 1, :, :]], -1)


def unpacked(block):
    half = block.shape[-1] // 2
    return jnp.stack([block[..., :half], block[..., half:]], -3)


def product(left, right):
    rows = left.shape[1]
    half = right.shape[-1] // 2
    both = jnp.matmul(left.reshape(2 * rows, left.shape[2]), right, precision=lax.Precision.HIGH)
    real = both[:rows, :half] - both[rows:, half:]
    imag = both[:rows, half:] + both[rows:, :half]
    return jnp.stack([real, imag])


def scaled(value, weight_re, weight_im):
    return jnp.stack(
        [value[0] * weight_re - value[1] * weight_im, value[0] * weight_im + value[1] * weight_re]
    )


def shards(diag_even, odd_green, lower, upper):
    rows = lower.shape[2]
    orbitals = lower.shape[3]
    wide = 2 * orbitals
    next_lower = shifted(lower[0], "slab", -1)
    mine = jnp.concatenate([packed(odd_green), packed(lower[1::2]), packed(upper[1::2])])
    whole = lax.all_gather(mine, "orb", axis=1, tiled=True)
    left_rows = (
        jnp.concatenate([upper[0], lower[2]], 1),
        jnp.concatenate([upper[2], next_lower], 1),
    )
    parts = []
    for odd in range(2):
        middle = product(left_rows[odd], whole[odd])
        parts.append((product(middle, whole[2 + odd]), product(middle, whole[4 + odd])))
    (first_down, first_up), (second_down, second_up) = parts
    kept_diag = diag_even[0] - first_down[:, :rows]
    kept_upper = -first_up[:, :rows]
    pivot_diag = diag_even[1] - first_up[:, rows:] - second_down[:, :rows]
    pivot_lower = -first_down[:, rows:]
    pivot_upper = -second_up[:, :rows]
    next_part = -second_up[:, rows:]
    next_kept_lower = -second_down[:, rows:]

    mine_two = jnp.concatenate([packed(pivot_diag), packed(pivot_lower), packed(pivot_upper)], -1)
    whole_two = gathered_by_permutes(mine_two)
    pivot = whole_two[:, :wide]
    on_diagonal = jnp.eye(orbitals, dtype=bool)
    diag_re = jnp.sum(jnp.where(on_diagonal, pivot[:, :orbitals], 0.0), axis=0)
    diag_im = jnp.sum(jnp.where(on_diagonal, pivot[:, orbitals:], 0.0), axis=0)
    modulus = diag_re * diag_re + diag_im * diag_im
    weight_re = (diag_re / modulus)[None, :]
    weight_im = (-diag_im / modulus)[None, :]

    def times_first(value):
        value = scaled(value, weight_re, weight_im)
        return 2.0 * value - scaled(product(value, pivot), weight_re, weight_im)

    chain = jnp.concatenate([kept_upper, next_kept_lower], 1)
    estimate = times_first(chain)
    solved = 2.0 * estimate - times_first(product(estimate, pivot))
    with_lower = product(solved, whole_two[:, wide : 2 * wide])
    with_upper = product(solved, whole_two[:, 2 * wide :])
    sent = jnp.stack([next_part - with_upper[:, rows:], -with_lower[:, rows:]])
    came = shifted(sent, "slab", 1)
    final_diag = kept_diag - with_lower[:, :rows] + came[0]
    final_upper = -with_upper[:, :rows]
    return final_diag[None], came[1][None], final_upper[None]


def solution(mesh):
    spec = P("slab", None, "orb", None)
    return jax.shard_map(
        shards, mesh=mesh, in_specs=(spec,) * 4, out_specs=(spec,) * 3, check_vma=False
    )
```

```python
import jax
import jax.numpy as jnp
from jax import lax
from jax.experimental import pallas as pl
from jax.experimental.pallas import tpu as pltpu
from jax.sharding import PartitionSpec as P

SIDE = 4
VMEM_LIMIT = 28 * 1024 * 1024


def permuted(value, slabs, target):
    pairs = []
    for slab in range(slabs):
        for line in range(SIDE):
            for kind in range(SIDE):
                there = target(slab, line, kind)
                if there is None:
                    continue
                to_slab, to_orb = there
                pairs.append((slab * SIDE * SIDE + orb(slab, line, kind), to_slab % slabs * SIDE * SIDE + to_orb))
    return lax.ppermute(value, ("slab", "orb"), pairs)


def orb(slab, line, kind):
    line, kind = line % SIDE, kind % SIDE
    return SIDE * kind + line if slab % 2 == 0 else SIDE * line + kind


def along_kind(step):
    return lambda slab, line, kind: (slab, orb(slab, line, kind + step))


def along_line(step):
    return lambda slab, line, kind: (slab, orb(slab, line + step, kind))


def crossed(slab, line, kind):
    return slab, orb(slab, line, kind ^ 2)


def outwards(slab, line, kind):
    return (slab, orb(slab, line, kind ^ 1)) if kind in (1, 2) else None


def inner(slab, line, kind):
    return (slab, orb(slab, line, 3 - kind)) if kind in (1, 2) else None


def slab_below(slab, line, kind):
    return slab - 1, orb(slab, line, kind)


def to_owner(step):
    def target(slab, line, kind):
        return slab + kind // 2, orb(slab, line, step + kind - line)

    return target


def place():
    core = lax.rem(lax.axis_index("slab"), 2)
    index = lax.axis_index("orb")
    y = lax.div(index, SIDE)
    x = lax.rem(index, SIDE)
    return core, jnp.where(core == 0, x, y), jnp.where(core == 0, y, x)


def block_row(core, line, step, block, rows):
    there = lax.rem(line - step + 4, 4)
    index = jnp.where(core == 0, SIDE * block + there, SIDE * there + block)
    return pl.multiple_of(index * rows, rows)


def halves(value):
    high = value.astype(jnp.bfloat16)
    low = (value - high.astype(jnp.float32)).astype(jnp.bfloat16)
    return high, low


def dot(first, second):
    return jnp.dot(first, second, preferred_element_type=jnp.float32)


def product(left_re, left_im, right_high, right_low):
    rows, width = left_re.shape
    high, low = halves(jnp.concatenate([left_re, left_im], 0))
    both = dot(high, right_high) + (dot(high, right_low) + dot(low, right_high))
    return (
        both[:rows, :width] - both[rows:, width:],
        both[:rows, width:] + both[rows:, :width],
    )


def store_block(high_ref, low_ref, row, rows, block_re, block_im):
    width = block_re.shape[1]
    for part, value in enumerate((block_re, block_im)):
        high, low = halves(value)
        columns = slice(part * width, (part + 1) * width)
        high_ref[pl.ds(row, rows), columns] = high
        low_ref[pl.ds(row, rows), columns] = low


def first_kernel(*refs):
    chunks = refs[0:4]
    lefts = refs[4:8]
    both_ref, term_ref, cross_ref = refs[8:11]
    green_high, green_low, part_high, part_low, left = refs[11:]
    core, line, kind = place()
    rows = lefts[0].shape[2]
    for step in range(4):
        for block in range(4):
            row = block_row(core, line, step, lax.rem(kind - block + 4, 4), rows)
            ref = chunks[step].at[block]
            store_block(green_high, green_low, row, rows, ref[0, 0], ref[0, 1])
            store_block(part_high, part_low, row, rows, ref[1, 0], ref[1, 1])
    for step in range(4):
        own = pl.multiple_of(lax.rem(kind - step + 4, 4) * rows, rows)
        for side in range(2):
            for part in range(2):
                left[part, pl.ds(side * 4 * rows + own, rows), :] = lefts[step][side, part]
    middle_re, middle_im = product(left[0], left[1], green_high[...], green_low[...])
    out_re, out_im = product(middle_re, middle_im, part_high[...], part_low[...])
    count = 4 * rows
    even = lax.rem(kind, 2) == 0
    outer = (kind == 0) | (kind == 3)
    for part, value in enumerate((out_re, out_im)):
        below = -value[:count]
        above = -value[count:]
        panel = jnp.where(even, above, below)
        other = jnp.where(even, below, above)
        for block in range(4):
            piece = slice(block * rows, (block + 1) * rows)
            both_ref[0, block, part] = panel[piece]
            term_ref[block, part] = other[piece]
        for step in range(4):
            block = lax.rem(kind - step + 4, 4)
            term_ref[block, part] += jnp.where(kind == 1, lefts[step][2, part], 0.0)
        for block in range(4):
            term = term_ref[block, part]
            both_ref[1, block, part] = term
            cross_ref[block, part] = jnp.where(outer, both_ref[0, block, part], term)


def second_kernel(*refs):
    left_ref, keep_ref = refs[0:2]
    pivots = refs[2:6]
    panels = refs[6:10]
    out_ref = refs[10]
    pivot_high, pivot_low, panel_high, panel_low = refs[11:]
    core, line, kind = place()
    rows = left_ref.shape[2]
    width = left_ref.shape[3]
    column_iota = lax.broadcasted_iota(jnp.int32, (rows, width), 1)
    row_iota = lax.broadcasted_iota(jnp.int32, (rows, width), 0)
    diag_re = jnp.zeros((1, width), jnp.float32)
    diag_im = jnp.zeros((1, width), jnp.float32)
    for step in range(4):
        for block in range(4):
            row = block_row(core, line, step, block, rows)
            block_re = pivots[step][block, 0]
            block_im = pivots[step][block, 1]
            on_diagonal = column_iota == row_iota + row
            diag_re += jnp.sum(jnp.where(on_diagonal, block_re, 0.0), axis=0, keepdims=True)
            diag_im += jnp.sum(jnp.where(on_diagonal, block_im, 0.0), axis=0, keepdims=True)
            store_block(pivot_high, pivot_low, row, rows, block_re, block_im)
            store_block(panel_high, panel_low, row, rows, panels[step][block, 0], panels[step][block, 1])
    modulus = diag_re * diag_re + diag_im * diag_im
    weight_re = diag_re / modulus
    weight_im = -diag_im / modulus

    def scaled(re, im):
        return re * weight_re - im * weight_im, re * weight_im + im * weight_re

    def times_pivot(re, im):
        return product(re, im, pivot_high[...], pivot_low[...])

    def times_first(re, im):
        re, im = scaled(re, im)
        take_re, take_im = scaled(*times_pivot(re, im))
        return 2.0 * re - take_re, 2.0 * im - take_im

    left_re = jnp.concatenate([left_ref[block, 0] for block in range(4)], 0)
    left_im = jnp.concatenate([left_ref[block, 1] for block in range(4)], 0)
    guess_re, guess_im = times_first(left_re, left_im)
    take_re, take_im = times_first(*times_pivot(guess_re, guess_im))
    solved_re = 2.0 * guess_re - take_re
    solved_im = 2.0 * guess_im - take_im
    outs = product(solved_re, solved_im, panel_high[...], panel_low[...])
    for part, value in enumerate(outs):
        for block in range(4):
            kept = jnp.where((kind == 0) | (kind == 3), keep_ref[block, part], 0.0)
            slot = lax.rem(block + line - kind + 4, 4)
            out_ref[slot, part] = kept - value[block * rows : (block + 1) * rows]


def vmem(count):
    return [pl.BlockSpec(memory_space=pltpu.VMEM)] * count


def shards(diag_even, odd_green, lower, upper):
    rows = lower.shape[2]
    width = lower.shape[3]
    slabs = lax.axis_size("slab")
    core, line, kind = place()
    next_lower = permuted(lower[0], slabs, slab_below)

    def wanted(step):
        code = lax.rem(kind + step, 4)
        return lax.div(code, 2), lax.rem(code, 2)

    def rights(step):
        odd, part = wanted(step)
        green = lax.dynamic_index_in_dim(odd_green, odd, 0, False)
        down = lax.dynamic_index_in_dim(lower, 2 * odd + 1, 0, False)
        up = lax.dynamic_index_in_dim(upper, 2 * odd + 1, 0, False)
        return jnp.stack([green, jnp.where(part == 0, down, up)])

    def lefts(step):
        odd, part = wanted(step)
        below = lax.dynamic_index_in_dim(upper, 2 * odd, 0, False)
        above = jnp.where(odd == 0, lower[2], next_lower)
        return jnp.stack([below, above, diag_even[1]])

    whole = jnp.stack([rights(0)] + [permuted(rights(step), slabs, along_kind(step)) for step in range(1, 4)])
    rings = [permuted(whole, slabs, along_line(step)) for step in range(1, 4)]
    left_rows = [lefts(0)] + [permuted(lefts(step), slabs, along_kind(step)) for step in range(1, 4)]
    four = jax.ShapeDtypeStruct((4, 2, rows, width), jnp.float32)
    wide = pltpu.VMEM((width, 2 * width), jnp.bfloat16)
    both, term, cross = pl.pallas_call(
        first_kernel,
        out_shape=[jax.ShapeDtypeStruct((2, 4, 2, rows, width), jnp.float32), four, four],
        in_specs=vmem(8),
        out_specs=vmem(3),
        scratch_shapes=[wide] * 4 + [pltpu.VMEM((2, 8 * rows, width), jnp.float32)],
        compiler_params=pltpu.CompilerParams(vmem_limit_bytes=VMEM_LIMIT),
        name="first_level",
    )(whole, *rings, *left_rows)

    outer = (kind == 0) | (kind == 3)
    cross_there = permuted(cross, slabs, crossed)
    both_there = permuted(both, slabs, outwards)
    term_there = permuted(term, slabs, inner)
    panel = jnp.where(outer, both[0], cross_there)
    panel_rings = [permuted(panel, slabs, along_line(step)) for step in range(1, 4)]
    pivot = jnp.where(outer, cross_there + both_there[1], term + term_there)
    pivot_rings = [permuted(pivot, slabs, along_line(step)) for step in range(1, 4)]
    left = jnp.where(outer, both_there[0], both[0])
    out = pl.pallas_call(
        second_kernel,
        out_shape=four,
        in_specs=vmem(10),
        out_specs=vmem(1)[0],
        scratch_shapes=[wide] * 4,
        compiler_params=pltpu.CompilerParams(vmem_limit_bytes=VMEM_LIMIT),
        name="second_level",
    )(left, term, pivot, *pivot_rings, panel, *panel_rings)
    ends = [permuted(out[step], slabs, to_owner(step)) for step in range(4)]

    def ended(code):
        place_of = lax.rem(line + kind - code + 4, 4)
        result = ends[0]
        for step in range(1, 4):
            result = jnp.where(place_of == step, ends[step], result)
        return result

    final_diag = diag_even[0] + ended(0) + ended(3)
    return final_diag[None], ended(2)[None], ended(1)[None]


def solution(mesh):
    spec = P("slab", None, "orb", None)
    return jax.shard_map(
        shards, mesh=mesh, in_specs=(spec,) * 4, out_specs=(spec,) * 3, check_vma=False
    )
```

```python
import jax
import jax.numpy as jnp
from jax import lax
from jax.experimental import pallas as pl
from jax.experimental.pallas import tpu as pltpu
from jax.sharding import PartitionSpec as P

SIDE = 4
VMEM_LIMIT = 20 * 1024 * 1024


def permuted(value, slabs, target):
    pairs = []
    for slab in range(slabs):
        for line in range(SIDE):
            for spot in range(SIDE):
                there = target(slab, line, spot)
                if there is None:
                    continue
                to_slab, to_orb = there
                pairs.append((slab * SIDE * SIDE + orb(slab, line, spot), to_slab % slabs * SIDE * SIDE + to_orb))
    return lax.ppermute(value, ("slab", "orb"), pairs)


def orb(slab, line, spot):
    line, spot = line % SIDE, spot % SIDE
    return SIDE * spot + line if slab % 2 == 0 else SIDE * line + spot


def along_spot(step):
    return lambda slab, line, spot: (slab, orb(slab, line, spot + step))


def along_line(step):
    return lambda slab, line, spot: (slab, orb(slab, line + step, spot))


def crossed(slab, line, spot):
    return slab, orb(slab, line, 3 - spot)


def outwards(slab, line, spot):
    return (slab, orb(slab, line, spot - 1)) if spot % 2 else None


def inner(slab, line, spot):
    return (slab, orb(slab, line, spot + 2)) if spot % 2 else None


def slab_below(slab, line, spot):
    return slab - 1, orb(slab, line, spot)


def to_owner(step):
    def target(slab, line, spot):
        return slab + spot // 2, orb(slab, line, step + spot - line)

    return target


def place():
    core = lax.rem(lax.axis_index("slab"), 2)
    index = lax.axis_index("orb")
    y = lax.div(index, SIDE)
    x = lax.rem(index, SIDE)
    return core, jnp.where(core == 0, x, y), jnp.where(core == 0, y, x)


def block_row(core, line, step, block, rows):
    there = lax.rem(line - step + 4, 4)
    index = jnp.where(core == 0, SIDE * block + there, SIDE * there + block)
    return pl.multiple_of(index * rows, rows)


def halves(value):
    high = value.astype(jnp.bfloat16)
    low = (value - high.astype(jnp.float32)).astype(jnp.bfloat16)
    return high, low


def dot(first, second):
    return jnp.dot(first, second, preferred_element_type=jnp.float32)


def product(left_re, left_im, right_high, right_low):
    rows, width = left_re.shape
    high, low = halves(jnp.concatenate([left_re, left_im], 0))
    both = dot(high, right_high) + (dot(high, right_low) + dot(low, right_high))
    return (
        both[:rows, :width] - both[rows:, width:],
        both[:rows, width:] + both[rows:, :width],
    )


def store_block(high_ref, low_ref, row, rows, block_re, block_im):
    width = block_re.shape[1]
    for part, value in enumerate((block_re, block_im)):
        high, low = halves(value)
        columns = slice(part * width, (part + 1) * width)
        high_ref[pl.ds(row, rows), columns] = high
        low_ref[pl.ds(row, rows), columns] = low


def first_kernel(*refs):
    messages = refs[0:4]
    rings = refs[4:7]
    front_ref, term_ref, cross_ref = refs[7:10]
    green_high, green_low, part_high, part_low, left = refs[10:]
    core, line, spot = place()
    rows = messages[0].shape[2]
    for step in range(4):
        for block in range(4):
            row = block_row(core, line, step, lax.rem(spot - block + 4, 4), rows)
            ref = messages[block] if step == 0 else rings[step - 1].at[block]
            store_block(green_high, green_low, row, rows, ref[0, 0], ref[0, 1])
            store_block(part_high, part_low, row, rows, ref[1, 0], ref[1, 1])
    for step in range(4):
        own = pl.multiple_of(lax.rem(spot - step + 4, 4) * rows, rows)
        for part in range(2):
            left[part, pl.ds(own, rows), :] = messages[step][2, part]
            left[part, pl.ds(4 * rows + own, rows), :] = messages[step][3, part]
    middle_re, middle_im = product(left[0], left[1], green_high[...], green_low[...])
    out_re, out_im = product(middle_re, middle_im, part_high[...], part_low[...])
    count = 4 * rows
    with_lower = (spot == 0) | (spot == 3)
    outer = lax.rem(spot, 2) == 0
    for part, value in enumerate((out_re, out_im)):
        below = -value[:count]
        above = -value[count:]
        panel = jnp.where(with_lower, above, below)
        other = jnp.where(with_lower, below, above)
        for block in range(4):
            piece = slice(block * rows, (block + 1) * rows)
            front_ref[block, part] = panel[piece]
            term_ref[block, part] = other[piece]
        for step in range(2):
            block = lax.rem(spot - step + 4, 4)
            term_ref[block, part] += jnp.where(outer, 0.0, messages[step][4, part])
        for block in range(4):
            cross_ref[block, part] = jnp.where(outer, front_ref[block, part], term_ref[block, part])


def second_kernel(*refs):
    front_ref, front_there_ref, keep_ref = refs[0:3]
    chunks = refs[3:7]
    out_ref = refs[7]
    pivot_high, pivot_low, panel_high, panel_low = refs[8:]
    core, line, spot = place()
    rows = front_ref.shape[2]
    width = front_ref.shape[3]
    outer = lax.rem(spot, 2) == 0
    column_iota = lax.broadcasted_iota(jnp.int32, (rows, width), 1)
    row_iota = lax.broadcasted_iota(jnp.int32, (rows, width), 0)
    diag_re = jnp.zeros((1, width), jnp.float32)
    diag_im = jnp.zeros((1, width), jnp.float32)
    for step in range(4):
        for block in range(4):
            row = block_row(core, line, step, block, rows)
            block_re = chunks[step][0, block, 0]
            block_im = chunks[step][0, block, 1]
            on_diagonal = column_iota == row_iota + row
            diag_re += jnp.sum(jnp.where(on_diagonal, block_re, 0.0), axis=0, keepdims=True)
            diag_im += jnp.sum(jnp.where(on_diagonal, block_im, 0.0), axis=0, keepdims=True)
            store_block(pivot_high, pivot_low, row, rows, block_re, block_im)
            store_block(panel_high, panel_low, row, rows, chunks[step][1, block, 0], chunks[step][1, block, 1])
    modulus = diag_re * diag_re + diag_im * diag_im
    weight_re = diag_re / modulus
    weight_im = -diag_im / modulus

    def scaled(re, im):
        return re * weight_re - im * weight_im, re * weight_im + im * weight_re

    def times_pivot(re, im):
        return product(re, im, pivot_high[...], pivot_low[...])

    def times_first(re, im):
        re, im = scaled(re, im)
        take_re, take_im = scaled(*times_pivot(re, im))
        return 2.0 * re - take_re, 2.0 * im - take_im

    left_re, left_im = (
        jnp.concatenate([jnp.where(outer, front_there_ref[block, part], front_ref[block, part]) for block in range(4)], 0)
        for part in range(2)
    )
    guess_re, guess_im = times_first(left_re, left_im)
    take_re, take_im = times_first(*times_pivot(guess_re, guess_im))
    solved_re = 2.0 * guess_re - take_re
    solved_im = 2.0 * guess_im - take_im
    outs = product(solved_re, solved_im, panel_high[...], panel_low[...])
    for part, value in enumerate(outs):
        for block in range(4):
            kept = jnp.where(outer, keep_ref[block, part], 0.0)
            slot = lax.rem(block + line - spot + 4, 4)
            out_ref[slot, part] = kept - value[block * rows : (block + 1) * rows]


def vmem(count):
    return [pl.BlockSpec(memory_space=pltpu.VMEM)] * count


def shards(diag_even, odd_green, lower, upper):
    rows = lower.shape[2]
    width = lower.shape[3]
    slabs = lax.axis_size("slab")
    core, line, spot = place()
    next_lower = permuted(lower[0], slabs, slab_below)

    def message(step):
        there = lax.rem(spot + step, 4)
        odd = lax.div(there, 2)
        green = lax.dynamic_index_in_dim(odd_green, odd, 0, False)
        down = lax.dynamic_index_in_dim(lower, 2 * odd + 1, 0, False)
        up = lax.dynamic_index_in_dim(upper, 2 * odd + 1, 0, False)
        below = lax.dynamic_index_in_dim(upper, 2 * odd, 0, False)
        with_lower = (there == 0) | (there == 3)
        above = jnp.where(odd == 0, lower[2], next_lower)
        blocks = [green, jnp.where(with_lower, down, up), below, above]
        return jnp.stack(blocks + [diag_even[1]] if step < 2 else blocks)

    def around(value, move, own):
        far, near, back = [permuted(value(step), slabs, move(step)) for step in (2, 1, 3)]
        return [own, near, far, back]

    messages = around(message, along_spot, message(0))
    whole = jnp.stack([piece[:2] for piece in messages])
    rings = around(lambda step: whole, along_line, whole)[1:]
    four = jax.ShapeDtypeStruct((4, 2, rows, width), jnp.float32)
    wide = pltpu.VMEM((width, 2 * width), jnp.bfloat16)
    front, term, cross = pl.pallas_call(
        first_kernel,
        out_shape=[four] * 3,
        in_specs=vmem(7),
        out_specs=vmem(3),
        scratch_shapes=[wide] * 4 + [pltpu.VMEM((2, 8 * rows, width), jnp.float32)],
        compiler_params=pltpu.CompilerParams(vmem_limit_bytes=VMEM_LIMIT),
        name="first_level",
    )(*messages, *rings)

    outer = lax.rem(spot, 2) == 0
    term_there = permuted(term, slabs, inner)
    term_out = permuted(term, slabs, outwards)
    cross_there = permuted(cross, slabs, crossed)
    panel = jnp.where(outer, front, cross_there)
    pivot = jnp.where(outer, cross_there + term_out, term + term_there)
    chunk = jnp.stack([pivot, panel])
    chunks = around(lambda step: chunk, along_line, chunk)
    after, _ = lax.optimization_barrier((front, term_there))
    front_there = permuted(after, slabs, outwards)
    out = pl.pallas_call(
        second_kernel,
        out_shape=four,
        in_specs=vmem(7),
        out_specs=vmem(1)[0],
        scratch_shapes=[wide] * 4,
        compiler_params=pltpu.CompilerParams(vmem_limit_bytes=VMEM_LIMIT),
        name="second_level",
    )(front, front_there, term, *chunks)
    ends = [permuted(out[step], slabs, to_owner(step)) for step in range(4)]

    def ended(code):
        place_of = lax.rem(line + spot - code + 4, 4)
        result = ends[0]
        for step in range(1, 4):
            result = jnp.where(place_of == step, ends[step], result)
        return result

    final_diag = diag_even[0] + ended(0) + ended(2)
    return final_diag[None], ended(3)[None], ended(1)[None]


def solution(mesh):
    spec = P("slab", None, "orb", None)
    return jax.shard_map(
        shards, mesh=mesh, in_specs=(spec,) * 4, out_specs=(spec,) * 3, check_vma=False
    )
```

```python
import jax
import jax.numpy as jnp
from jax import lax
from jax.experimental import pallas as pl
from jax.experimental.pallas import tpu as pltpu
from jax.sharding import PartitionSpec as P

SIDE = 4
VMEM_LIMIT = 20 * 1024 * 1024


def permuted(value, slabs, target):
    pairs = []
    for slab in range(slabs):
        for line in range(SIDE):
            for spot in range(SIDE):
                there = target(slab, line, spot)
                if there is None:
                    continue
                to_slab, to_orb = there
                pairs.append((slab * SIDE * SIDE + orb(slab, line, spot), to_slab % slabs * SIDE * SIDE + to_orb))
    return lax.ppermute(value, ("slab", "orb"), pairs)


def orb(slab, line, spot):
    line, spot = line % SIDE, spot % SIDE
    return SIDE * spot + line if slab % 2 == 0 else SIDE * line + spot


def along_spot(step):
    return lambda slab, line, spot: (slab, orb(slab, line, spot + step))


def along_line(step):
    return lambda slab, line, spot: (slab, orb(slab, line + step, spot))


def crossed(slab, line, spot):
    return slab, orb(slab, line, 3 - spot)


def outwards(slab, line, spot):
    return (slab, orb(slab, line, spot - 1)) if spot % 2 else None


def inner(slab, line, spot):
    return (slab, orb(slab, line, spot + 2)) if spot % 2 else None


def slab_below(slab, line, spot):
    return slab - 1, orb(slab, line, spot)


def to_owner(step):
    def target(slab, line, spot):
        return slab + spot // 2, orb(slab, line, step + spot - line)

    return target


def place():
    core = lax.rem(lax.axis_index("slab"), 2)
    index = lax.axis_index("orb")
    y = lax.div(index, SIDE)
    x = lax.rem(index, SIDE)
    return core, jnp.where(core == 0, x, y), jnp.where(core == 0, y, x)


def block_row(core, line, step, block, rows):
    there = lax.rem(line - step + 4, 4)
    index = jnp.where(core == 0, SIDE * block + there, SIDE * there + block)
    return pl.multiple_of(index * rows, rows)


def halves(value):
    high = value.astype(jnp.bfloat16)
    low = (value - high.astype(jnp.float32)).astype(jnp.bfloat16)
    return high, low


def dot(first, second):
    return jnp.dot(first, second, preferred_element_type=jnp.float32)


def product(left_re, left_im, right_high, right_low):
    rows, width = left_re.shape
    high, low = halves(jnp.concatenate([left_re, left_im], 0))
    both = dot(high, right_high) + (dot(high, right_low) + dot(low, right_high))
    return (
        both[:rows, :width] - both[rows:, width:],
        both[:rows, width:] + both[rows:, :width],
    )


def store_block(high_ref, low_ref, row, rows, block_re, block_im):
    width = block_re.shape[1]
    for part, value in enumerate((block_re, block_im)):
        high, low = halves(value)
        columns = slice(part * width, (part + 1) * width)
        high_ref[pl.ds(row, rows), columns] = high
        low_ref[pl.ds(row, rows), columns] = low


def first_kernel(*refs):
    messages = refs[0:4]
    greens = refs[4:7]
    parts = refs[7:10]
    front_ref, term_ref, cross_ref = refs[10:13]
    green_high, green_low, part_high, part_low, left = refs[13:]
    core, line, spot = place()
    rows = messages[0].shape[2]
    for step in range(4):
        for block in range(4):
            row = block_row(core, line, step, lax.rem(spot - block + 4, 4), rows)
            green = messages[block].at[0] if step == 0 else greens[step - 1].at[block]
            factor = messages[block].at[1] if step == 0 else parts[step - 1].at[block]
            store_block(green_high, green_low, row, rows, green[0], green[1])
            store_block(part_high, part_low, row, rows, factor[0], factor[1])
    for step in range(4):
        own = pl.multiple_of(lax.rem(spot - step + 4, 4) * rows, rows)
        for part in range(2):
            left[part, pl.ds(own, rows), :] = messages[step][2, part]
            left[part, pl.ds(4 * rows + own, rows), :] = messages[step][3, part]
    middle_re, middle_im = product(left[0], left[1], green_high[...], green_low[...])
    out_re, out_im = product(middle_re, middle_im, part_high[...], part_low[...])
    count = 4 * rows
    with_lower = (spot == 0) | (spot == 3)
    outer = lax.rem(spot, 2) == 0
    for part, value in enumerate((out_re, out_im)):
        below = -value[:count]
        above = -value[count:]
        panel = jnp.where(with_lower, above, below)
        other = jnp.where(with_lower, below, above)
        for block in range(4):
            piece = slice(block * rows, (block + 1) * rows)
            front_ref[block, part] = panel[piece]
            term_ref[block, part] = other[piece]
        for step in (0, 3):
            block = lax.rem(spot - step + 4, 4)
            term_ref[block, part] += jnp.where(outer, 0.0, messages[step][4, part])
        for block in range(4):
            cross_ref[block, part] = jnp.where(outer, front_ref[block, part], term_ref[block, part])


def second_kernel(*refs):
    front_ref, front_there_ref, keep_ref = refs[0:3]
    pivots = refs[3:7]
    panels = refs[7:11]
    out_ref = refs[11]
    pivot_high, pivot_low, panel_high, panel_low = refs[12:]
    core, line, spot = place()
    rows = front_ref.shape[2]
    width = front_ref.shape[3]
    outer = lax.rem(spot, 2) == 0
    column_iota = lax.broadcasted_iota(jnp.int32, (rows, width), 1)
    row_iota = lax.broadcasted_iota(jnp.int32, (rows, width), 0)
    diag_re = jnp.zeros((1, width), jnp.float32)
    diag_im = jnp.zeros((1, width), jnp.float32)
    for step in range(4):
        for block in range(4):
            row = block_row(core, line, step, block, rows)
            block_re = pivots[step][block, 0]
            block_im = pivots[step][block, 1]
            on_diagonal = column_iota == row_iota + row
            diag_re += jnp.sum(jnp.where(on_diagonal, block_re, 0.0), axis=0, keepdims=True)
            diag_im += jnp.sum(jnp.where(on_diagonal, block_im, 0.0), axis=0, keepdims=True)
            store_block(pivot_high, pivot_low, row, rows, block_re, block_im)
            store_block(panel_high, panel_low, row, rows, panels[step][block, 0], panels[step][block, 1])
    modulus = diag_re * diag_re + diag_im * diag_im
    weight_re = diag_re / modulus
    weight_im = -diag_im / modulus

    def scaled(re, im):
        return re * weight_re - im * weight_im, re * weight_im + im * weight_re

    def times_pivot(re, im):
        return product(re, im, pivot_high[...], pivot_low[...])

    def times_first(re, im):
        re, im = scaled(re, im)
        take_re, take_im = scaled(*times_pivot(re, im))
        return 2.0 * re - take_re, 2.0 * im - take_im

    left_re, left_im = (
        jnp.concatenate([jnp.where(outer, front_there_ref[block, part], front_ref[block, part]) for block in range(4)], 0)
        for part in range(2)
    )
    guess_re, guess_im = times_first(left_re, left_im)
    take_re, take_im = times_first(*times_pivot(guess_re, guess_im))
    solved_re = 2.0 * guess_re - take_re
    solved_im = 2.0 * guess_im - take_im
    outs = product(solved_re, solved_im, panel_high[...], panel_low[...])
    for part, value in enumerate(outs):
        for block in range(4):
            kept = jnp.where(outer, keep_ref[block, part], 0.0)
            slot = lax.rem(block + line - spot + 4, 4)
            out_ref[slot, part] = kept - value[block * rows : (block + 1) * rows]


def vmem(count):
    return [pl.BlockSpec(memory_space=pltpu.VMEM)] * count


def shards(diag_even, odd_green, lower, upper):
    rows = lower.shape[2]
    width = lower.shape[3]
    slabs = lax.axis_size("slab")
    core, line, spot = place()
    next_lower = permuted(lower[0], slabs, slab_below)

    def message(step):
        there = lax.rem(spot + step, 4)
        odd = lax.div(there, 2)
        green = lax.dynamic_index_in_dim(odd_green, odd, 0, False)
        down = lax.dynamic_index_in_dim(lower, 2 * odd + 1, 0, False)
        up = lax.dynamic_index_in_dim(upper, 2 * odd + 1, 0, False)
        below = lax.dynamic_index_in_dim(upper, 2 * odd, 0, False)
        with_lower = (there == 0) | (there == 3)
        above = jnp.where(odd == 0, lower[2], next_lower)
        blocks = [green, jnp.where(with_lower, down, up), below, above]
        return jnp.stack(blocks + [diag_even[1]] if step in (0, 3) else blocks)

    def ringed(first, second):
        first_one = permuted(first, slabs, along_line(1))
        second_three = permuted(second, slabs, along_line(-1))
        first_two = permuted(first_one, slabs, along_line(1))
        second_two = permuted(second_three, slabs, along_line(-1))
        second_one = permuted(second, slabs, along_line(1))
        first_three = permuted(first, slabs, along_line(-1))
        return [first_one, first_two, first_three], [second_one, second_two, second_three]

    messages = [message(0)] + [permuted(message(step), slabs, along_spot(step)) for step in range(1, 4)]
    greens, parts = ringed(*(jnp.stack([piece[side] for piece in messages]) for side in range(2)))
    four = jax.ShapeDtypeStruct((4, 2, rows, width), jnp.float32)
    wide = pltpu.VMEM((width, 2 * width), jnp.bfloat16)
    front, term, cross = pl.pallas_call(
        first_kernel,
        out_shape=[four] * 3,
        in_specs=vmem(10),
        out_specs=vmem(3),
        scratch_shapes=[wide] * 4 + [pltpu.VMEM((2, 8 * rows, width), jnp.float32)],
        compiler_params=pltpu.CompilerParams(vmem_limit_bytes=VMEM_LIMIT),
        name="first_level",
    )(*messages, *greens, *parts)

    outer = lax.rem(spot, 2) == 0
    term_there = permuted(term, slabs, inner)
    term_out = permuted(term, slabs, outwards)
    cross_there = permuted(cross, slabs, crossed)
    panel = jnp.where(outer, front, cross_there)
    pivot = jnp.where(outer, cross_there + term_out, term + term_there)
    pivots, panels = ringed(pivot, panel)
    after, _ = lax.optimization_barrier((front, term_there))
    front_there = permuted(after, slabs, outwards)
    out = pl.pallas_call(
        second_kernel,
        out_shape=four,
        in_specs=vmem(11),
        out_specs=vmem(1)[0],
        scratch_shapes=[wide] * 4,
        compiler_params=pltpu.CompilerParams(vmem_limit_bytes=VMEM_LIMIT),
        name="second_level",
    )(front, front_there, term, pivot, *pivots, panel, *panels)
    ends = [permuted(out[step], slabs, to_owner(step)) for step in range(4)]

    def ended(code):
        place_of = lax.rem(line + spot - code + 4, 4)
        result = ends[0]
        for step in range(1, 4):
            result = jnp.where(place_of == step, ends[step], result)
        return result

    final_diag = diag_even[0] + ended(0) + ended(2)
    return final_diag[None], ended(3)[None], ended(1)[None]


def solution(mesh):
    spec = P("slab", None, "orb", None)
    return jax.shard_map(
        shards, mesh=mesh, in_specs=(spec,) * 4, out_specs=(spec,) * 3, check_vma=False
    )
```

```python
import jax
import jax.numpy as jnp
from jax import lax
from jax.experimental import pallas as pl
from jax.experimental.pallas import tpu as pltpu
from jax.sharding import PartitionSpec as P

SIDE = 4
VMEM_LIMIT = 20 * 1024 * 1024


def permuted(value, slabs, target):
    pairs = []
    for slab in range(slabs):
        for line in range(SIDE):
            for spot in range(SIDE):
                there = target(slab, line, spot)
                if there is None:
                    continue
                to_slab, to_orb = there
                pairs.append((slab * SIDE * SIDE + orb(slab, line, spot), to_slab % slabs * SIDE * SIDE + to_orb))
    return lax.ppermute(value, ("slab", "orb"), pairs)


def orb(slab, line, spot):
    line, spot = line % SIDE, spot % SIDE
    return SIDE * spot + line if slab % 2 == 0 else SIDE * line + spot


def along_spot(step):
    return lambda slab, line, spot: (slab, orb(slab, line, spot + step))


def along_line(step):
    return lambda slab, line, spot: (slab, orb(slab, line + step, spot))


def crossed(slab, line, spot):
    return slab, orb(slab, line, 3 - spot)


def outwards(slab, line, spot):
    return (slab, orb(slab, line, spot - 1)) if spot % 2 else None


def inner(slab, line, spot):
    return (slab, orb(slab, line, spot + 2)) if spot % 2 else None


def to_owner(step):
    def target(slab, line, spot):
        return slab + spot // 2, orb(slab, line, step + spot - line)

    return target


def from_owner(step):
    def target(slab, line, spot):
        code = (line + spot - step) % 4
        return (slab, orb(slab, line, code)) if code < 2 else (slab - 1, orb(slab - 1, spot, code))

    return target


def place():
    core = lax.rem(lax.axis_index("slab"), 2)
    index = lax.axis_index("orb")
    y = lax.div(index, SIDE)
    x = lax.rem(index, SIDE)
    return core, jnp.where(core == 0, x, y), jnp.where(core == 0, y, x)


def block_row(core, line, step, block, rows):
    there = lax.rem(line - step + 4, 4)
    index = jnp.where(core == 0, SIDE * block + there, SIDE * there + block)
    return pl.multiple_of(index * rows, rows)


def halves(value):
    high = value.astype(jnp.bfloat16)
    low = (value - high.astype(jnp.float32)).astype(jnp.bfloat16)
    return high, low


def dot(first, second):
    return jnp.dot(first, second, preferred_element_type=jnp.float32)


def product(left_re, left_im, right_high, right_low):
    rows, width = left_re.shape
    high, low = halves(jnp.concatenate([left_re, left_im], 0))
    both = dot(high, right_high) + (dot(high, right_low) + dot(low, right_high))
    return (
        both[:rows, :width] - both[rows:, width:],
        both[:rows, width:] + both[rows:, :width],
    )


def store_block(high_ref, low_ref, row, rows, block_re, block_im):
    width = block_re.shape[1]
    for part, value in enumerate((block_re, block_im)):
        high, low = halves(value)
        columns = slice(part * width, (part + 1) * width)
        high_ref[pl.ds(row, rows), columns] = high
        low_ref[pl.ds(row, rows), columns] = low


def first_kernel(*refs):
    messages = refs[0:4]
    aboves = refs[4:8]
    greens = refs[8:11]
    parts = refs[11:14]
    front_ref, term_ref, cross_ref = refs[14:17]
    green_high, green_low, part_high, part_low, left = refs[17:]
    core, line, spot = place()
    rows = messages[0].shape[2]
    for step in range(4):
        for block in range(4):
            row = block_row(core, line, step, lax.rem(spot - block + 4, 4), rows)
            green = messages[block].at[0] if step == 0 else greens[step - 1].at[block]
            factor = messages[block].at[1] if step == 0 else parts[step - 1].at[block]
            store_block(green_high, green_low, row, rows, green[0], green[1])
            store_block(part_high, part_low, row, rows, factor[0], factor[1])
    for step in range(4):
        own = pl.multiple_of(lax.rem(spot - step + 4, 4) * rows, rows)
        there = pl.multiple_of(lax.rem(step + spot - line + 4, 4) * rows, rows)
        for part in range(2):
            left[part, pl.ds(own, rows), :] = messages[step][2, part]
            left[part, pl.ds(4 * rows + there, rows), :] = aboves[step][part]
    middle_re, middle_im = product(left[0], left[1], green_high[...], green_low[...])
    out_re, out_im = product(middle_re, middle_im, part_high[...], part_low[...])
    count = 4 * rows
    with_lower = (spot == 0) | (spot == 3)
    outer = lax.rem(spot, 2) == 0
    for part, value in enumerate((out_re, out_im)):
        below = -value[:count]
        above = -value[count:]
        panel = jnp.where(with_lower, above, below)
        other = jnp.where(with_lower, below, above)
        for block in range(4):
            piece = slice(block * rows, (block + 1) * rows)
            front_ref[block, part] = panel[piece]
            term_ref[block, part] = other[piece]
        for step in (0, 3):
            block = lax.rem(spot - step + 4, 4)
            term_ref[block, part] += jnp.where(outer, 0.0, messages[step][3, part])
        for block in range(4):
            cross_ref[block, part] = jnp.where(outer, front_ref[block, part], term_ref[block, part])


def second_kernel(*refs):
    front_ref, front_there_ref, keep_ref = refs[0:3]
    pivots = refs[3:7]
    panels = refs[7:11]
    out_ref = refs[11]
    pivot_high, pivot_low, panel_high, panel_low = refs[12:]
    core, line, spot = place()
    rows = front_ref.shape[2]
    width = front_ref.shape[3]
    outer = lax.rem(spot, 2) == 0
    column_iota = lax.broadcasted_iota(jnp.int32, (rows, width), 1)
    row_iota = lax.broadcasted_iota(jnp.int32, (rows, width), 0)
    diag_re = jnp.zeros((1, width), jnp.float32)
    diag_im = jnp.zeros((1, width), jnp.float32)
    for step in range(4):
        for block in range(4):
            row = block_row(core, line, step, block, rows)
            block_re = pivots[step][block, 0]
            block_im = pivots[step][block, 1]
            on_diagonal = column_iota == row_iota + row
            diag_re += jnp.sum(jnp.where(on_diagonal, block_re, 0.0), axis=0, keepdims=True)
            diag_im += jnp.sum(jnp.where(on_diagonal, block_im, 0.0), axis=0, keepdims=True)
            store_block(pivot_high, pivot_low, row, rows, block_re, block_im)
            store_block(panel_high, panel_low, row, rows, panels[step][block, 0], panels[step][block, 1])
    modulus = diag_re * diag_re + diag_im * diag_im
    weight_re = diag_re / modulus
    weight_im = -diag_im / modulus

    def scaled(re, im):
        return re * weight_re - im * weight_im, re * weight_im + im * weight_re

    def times_pivot(re, im):
        return product(re, im, pivot_high[...], pivot_low[...])

    def times_first(re, im):
        re, im = scaled(re, im)
        take_re, take_im = scaled(*times_pivot(re, im))
        return 2.0 * re - take_re, 2.0 * im - take_im

    left_re, left_im = (
        jnp.concatenate([jnp.where(outer, front_there_ref[block, part], front_ref[block, part]) for block in range(4)], 0)
        for part in range(2)
    )
    guess_re, guess_im = times_first(left_re, left_im)
    take_re, take_im = times_first(*times_pivot(guess_re, guess_im))
    solved_re = 2.0 * guess_re - take_re
    solved_im = 2.0 * guess_im - take_im
    outs = product(solved_re, solved_im, panel_high[...], panel_low[...])
    for part, value in enumerate(outs):
        for block in range(4):
            kept = jnp.where(outer, keep_ref[block, part], 0.0)
            slot = lax.rem(block + line - spot + 4, 4)
            out_ref[slot, part] = kept - value[block * rows : (block + 1) * rows]


def vmem(count):
    return [pl.BlockSpec(memory_space=pltpu.VMEM)] * count


def shards(diag_even, odd_green, lower, upper):
    rows = lower.shape[2]
    width = lower.shape[3]
    slabs = lax.axis_size("slab")
    core, line, spot = place()
    def message(step):
        there = lax.rem(spot + step, 4)
        odd = lax.div(there, 2)
        green = lax.dynamic_index_in_dim(odd_green, odd, 0, False)
        down = lax.dynamic_index_in_dim(lower, 2 * odd + 1, 0, False)
        up = lax.dynamic_index_in_dim(upper, 2 * odd + 1, 0, False)
        below = lax.dynamic_index_in_dim(upper, 2 * odd, 0, False)
        with_lower = (there == 0) | (there == 3)
        blocks = [green, jnp.where(with_lower, down, up), below]
        return jnp.stack(blocks + [diag_even[1]] if step in (0, 3) else blocks)

    def ringed(first, second):
        first_one = permuted(first, slabs, along_line(1))
        second_three = permuted(second, slabs, along_line(-1))
        first_two = permuted(first_one, slabs, along_line(1))
        second_two = permuted(second_three, slabs, along_line(-1))
        second_one = permuted(second, slabs, along_line(1))
        first_three = permuted(first, slabs, along_line(-1))
        return [first_one, first_two, first_three], [second_one, second_two, second_three]

    messages = [message(0)] + [permuted(message(step), slabs, along_spot(step)) for step in range(1, 4)]
    first, second = (jnp.stack([piece[side] for piece in messages]) for side in range(2))
    greens, parts = ringed(first, second)
    own_row, next_row, _ = lax.optimization_barrier((lower[2], lower[0], greens[0]))

    def above(step):
        return jnp.where(lax.rem(line + spot - step + 4, 4) < 2, own_row, next_row)

    aboves = [permuted(above(step), slabs, from_owner(step)) for step in range(4)]
    four = jax.ShapeDtypeStruct((4, 2, rows, width), jnp.float32)
    wide = pltpu.VMEM((width, 2 * width), jnp.bfloat16)
    front, term, cross = pl.pallas_call(
        first_kernel,
        out_shape=[four] * 3,
        in_specs=vmem(14),
        out_specs=vmem(3),
        scratch_shapes=[wide] * 4 + [pltpu.VMEM((2, 8 * rows, width), jnp.float32)],
        compiler_params=pltpu.CompilerParams(vmem_limit_bytes=VMEM_LIMIT),
        name="first_level",
    )(*messages, *aboves, *greens, *parts)

    outer = lax.rem(spot, 2) == 0
    term_there = permuted(term, slabs, inner)
    term_out = permuted(term, slabs, outwards)
    cross_there = permuted(cross, slabs, crossed)
    panel = jnp.where(outer, front, cross_there)
    pivot = jnp.where(outer, cross_there + term_out, term + term_there)
    pivots, panels = ringed(pivot, panel)
    after, _ = lax.optimization_barrier((front, term_there))
    front_there = permuted(after, slabs, outwards)
    out = pl.pallas_call(
        second_kernel,
        out_shape=four,
        in_specs=vmem(11),
        out_specs=vmem(1)[0],
        scratch_shapes=[wide] * 4,
        compiler_params=pltpu.CompilerParams(vmem_limit_bytes=VMEM_LIMIT),
        name="second_level",
    )(front, front_there, term, pivot, *pivots, panel, *panels)
    ends = [permuted(out[step], slabs, to_owner(step)) for step in range(4)]

    def ended(code):
        place_of = lax.rem(line + spot - code + 4, 4)
        result = ends[0]
        for step in range(1, 4):
            result = jnp.where(place_of == step, ends[step], result)
        return result

    final_diag = diag_even[0] + ended(0) + ended(2)
    return final_diag[None], ended(3)[None], ended(1)[None]


def solution(mesh):
    spec = P("slab", None, "orb", None)
    return jax.shard_map(
        shards, mesh=mesh, in_specs=(spec,) * 4, out_specs=(spec,) * 3, check_vma=False
    )
```

```python
import functools

import jax
import jax.numpy as jnp
from jax import lax
from jax.experimental import pallas as pl
from jax.experimental.pallas import tpu as pltpu
from jax.sharding import PartitionSpec as P

SIDE = 4
VMEM_LIMIT = 16 * 1024 * 1024


def permuted(value, slabs, target):
    pairs = []
    for slab in range(slabs):
        for line in range(SIDE):
            for spot in range(SIDE):
                there = target(slab, line, spot)
                if there is None:
                    continue
                to_slab, to_orb = there
                pairs.append((slab * SIDE * SIDE + orb(slab, line, spot), to_slab % slabs * SIDE * SIDE + to_orb))
    return lax.ppermute(value, ("slab", "orb"), pairs)


def orb(slab, line, spot):
    line, spot = line % SIDE, spot % SIDE
    return SIDE * spot + line if slab % 2 == 0 else SIDE * line + spot


def along_spot(step):
    return lambda slab, line, spot: (slab, orb(slab, line, spot + step))


def along_line(step):
    return lambda slab, line, spot: (slab, orb(slab, line + step, spot))


def crossed(slab, line, spot):
    return slab, orb(slab, line, 3 - spot)


def outwards(slab, line, spot):
    return (slab, orb(slab, line, spot - 1)) if spot % 2 else None


def inner(slab, line, spot):
    return (slab, orb(slab, line, spot + 2)) if spot % 2 else None


def to_owner(step):
    def target(slab, line, spot):
        return slab + spot // 2, orb(slab, line, step + spot - line)

    return target


def slab_below(slab, line, spot):
    return slab - 1, orb(slab, line, spot)


def place():
    core = lax.rem(lax.axis_index("slab"), 2)
    index = lax.axis_index("orb")
    y = lax.div(index, SIDE)
    x = lax.rem(index, SIDE)
    return core, jnp.where(core == 0, x, y), jnp.where(core == 0, y, x)


def block_row(core, line, step, block, rows):
    there = lax.rem(line - step + 4, 4)
    index = jnp.where(core == 0, SIDE * block + there, SIDE * there + block)
    return pl.multiple_of(index * rows, rows)


def halves(value):
    high = value.astype(jnp.bfloat16)
    low = (value - high.astype(jnp.float32)).astype(jnp.bfloat16)
    return high, low


def dot(first, second):
    return jnp.dot(first, second, preferred_element_type=jnp.float32)


def product(left_re, left_im, right_high, right_low):
    rows, width = left_re.shape
    high, low = halves(jnp.concatenate([left_re, left_im], 0))
    both = dot(high, right_high) + (dot(high, right_low) + dot(low, right_high))
    return (
        both[:rows, :width] - both[rows:, width:],
        both[:rows, width:] + both[rows:, :width],
    )


def store_block(high_ref, low_ref, row, rows, block_re, block_im):
    width = block_re.shape[1]
    for part, value in enumerate((block_re, block_im)):
        high, low = halves(value)
        columns = slice(part * width, (part + 1) * width)
        high_ref[pl.ds(row, rows), columns] = high
        low_ref[pl.ds(row, rows), columns] = low


def first_kernel(with_diag, *refs):
    messages = refs[0:4]
    greens = refs[4:7]
    parts = refs[7:10]
    lefts = refs[10:-6]
    out_ref = refs[-6]
    green_high, green_low, part_high, part_low, left = refs[-5:]
    core, line, spot = place()
    rows = messages[0].shape[2]
    for step in range(4):
        for block in range(4):
            row = block_row(core, line, step, lax.rem(spot - block + 4, 4), rows)
            green = messages[block].at[0] if step == 0 else greens[step - 1].at[block]
            factor = messages[block].at[1] if step == 0 else parts[step - 1].at[block]
            store_block(green_high, green_low, row, rows, green[0], green[1])
            store_block(part_high, part_low, row, rows, factor[0], factor[1])
    for step in range(4):
        own = pl.multiple_of(lax.rem(spot - step + 4, 4) * rows, rows)
        for part in range(2):
            left[part, pl.ds(own, rows), :] = messages[step][2, part] if with_diag else lefts[step][part]
    middle_re, middle_im = product(left[0], left[1], green_high[...], green_low[...])
    outs = product(middle_re, middle_im, part_high[...], part_low[...])
    for part, value in enumerate(outs):
        for block in range(4):
            out_ref[block, part] = -value[block * rows : (block + 1) * rows]
        if with_diag:
            for step in (0, 3):
                block = lax.rem(spot - step + 4, 4)
                diag = messages[step][3, part]
                out_ref[block, part] += jnp.where(lax.rem(spot, 2) == 0, 0.0, diag)


def second_kernel(*refs):
    side_ref, side_there_ref = refs[0:2]
    pivots = refs[2:6]
    panels = refs[6:10]
    out_ref = refs[10]
    pivot_high, pivot_low, panel_high, panel_low = refs[11:]
    core, line, spot = place()
    rows = side_ref.shape[2]
    width = side_ref.shape[3]
    outer = lax.rem(spot, 2) == 0
    column_iota = lax.broadcasted_iota(jnp.int32, (rows, width), 1)
    row_iota = lax.broadcasted_iota(jnp.int32, (rows, width), 0)
    diag_re = jnp.zeros((1, width), jnp.float32)
    diag_im = jnp.zeros((1, width), jnp.float32)
    for step in range(4):
        for block in range(4):
            row = block_row(core, line, step, block, rows)
            block_re = pivots[step][block, 0]
            block_im = pivots[step][block, 1]
            on_diagonal = column_iota == row_iota + row
            diag_re += jnp.sum(jnp.where(on_diagonal, block_re, 0.0), axis=0, keepdims=True)
            diag_im += jnp.sum(jnp.where(on_diagonal, block_im, 0.0), axis=0, keepdims=True)
            store_block(pivot_high, pivot_low, row, rows, block_re, block_im)
            store_block(panel_high, panel_low, row, rows, panels[step][block, 0], panels[step][block, 1])
    modulus = diag_re * diag_re + diag_im * diag_im
    weight_re = diag_re / modulus
    weight_im = -diag_im / modulus

    def scaled(re, im):
        return re * weight_re - im * weight_im, re * weight_im + im * weight_re

    def times_pivot(re, im):
        return product(re, im, pivot_high[...], pivot_low[...])

    def times_first(re, im):
        re, im = scaled(re, im)
        take_re, take_im = scaled(*times_pivot(re, im))
        return 2.0 * re - take_re, 2.0 * im - take_im

    left_re, left_im = (
        jnp.concatenate([jnp.where(outer, side_there_ref[block, part], side_ref[block, part]) for block in range(4)], 0)
        for part in range(2)
    )
    guess_re, guess_im = times_first(left_re, left_im)
    take_re, take_im = times_first(*times_pivot(guess_re, guess_im))
    solved_re = 2.0 * guess_re - take_re
    solved_im = 2.0 * guess_im - take_im
    outs = product(solved_re, solved_im, panel_high[...], panel_low[...])
    for part, value in enumerate(outs):
        for block in range(4):
            kept = jnp.where(outer, side_ref[block, part], 0.0)
            slot = lax.rem(block + line - spot + 4, 4)
            out_ref[slot, part] = kept - value[block * rows : (block + 1) * rows]


def vmem(count):
    return [pl.BlockSpec(memory_space=pltpu.VMEM)] * count


def shards(diag_even, odd_green, lower, upper):
    rows = lower.shape[2]
    width = lower.shape[3]
    slabs = lax.axis_size("slab")
    core, line, spot = place()
    def message(step):
        there = lax.rem(spot + step, 4)
        odd = lax.div(there, 2)
        green = lax.dynamic_index_in_dim(odd_green, odd, 0, False)
        down = lax.dynamic_index_in_dim(lower, 2 * odd + 1, 0, False)
        up = lax.dynamic_index_in_dim(upper, 2 * odd + 1, 0, False)
        with_lower = (there == 0) | (there == 3)
        blocks = [green, jnp.where(with_lower, down, up), jnp.where(odd == 0, lower[2], upper[2])]
        return jnp.stack(blocks + [diag_even[1]] if step in (0, 3) else blocks)

    def ringed(first, second):
        first_one = permuted(first, slabs, along_line(1))
        second_three = permuted(second, slabs, along_line(-1))
        first_two = permuted(first_one, slabs, along_line(1))
        second_two = permuted(second_three, slabs, along_line(-1))
        second_one = permuted(second, slabs, along_line(1))
        first_three = permuted(first, slabs, along_line(-1))
        return [first_one, first_two, first_three], [second_one, second_two, second_three]

    messages = [message(0)] + [permuted(message(step), slabs, along_spot(step)) for step in range(1, 4)]
    first, second = (jnp.stack([piece[side] for piece in messages]) for side in range(2))
    greens, parts = ringed(first, second)
    own_row, next_row, _ = lax.optimization_barrier((upper[0], lower[0], greens[0]))
    next_row = permuted(next_row, slabs, slab_below)
    four = jax.ShapeDtypeStruct((4, 2, rows, width), jnp.float32)
    wide = pltpu.VMEM((width, 2 * width), jnp.bfloat16)

    def rows_through(with_diag, message, lefts):
        flops = 3 * 2 * 2 * (8 * rows) * width * (2 * width)
        return pl.pallas_call(
            functools.partial(first_kernel, with_diag),
            out_shape=four,
            in_specs=vmem(10 + len(lefts)),
            out_specs=vmem(1)[0],
            scratch_shapes=[wide] * 4 + [pltpu.VMEM((2, 4 * rows, width), jnp.float32)],
            compiler_params=pltpu.CompilerParams(vmem_limit_bytes=VMEM_LIMIT),
            cost_estimate=pl.CostEstimate(flops=flops, bytes_accessed=12 * width * width, transcendentals=0),
            name="first_level" if with_diag else "first_level_side",
        )(message, *messages[1:], *greens, *parts, *lefts)

    ready, next_row = lax.optimization_barrier((messages[0], next_row))
    main = rows_through(True, ready, [])

    def late(step):
        return jnp.where(lax.rem(spot + step, 4) < 2, own_row, next_row)

    lates = [late(0)] + [permuted(late(step), slabs, along_spot(step)) for step in range(1, 4)]

    outer = lax.rem(spot, 2) == 0
    cross_there = permuted(main, slabs, crossed)
    term_out = permuted(main, slabs, outwards)
    term_there = permuted(main, slabs, inner)
    panel = jnp.where(outer, main, cross_there)
    pivot = jnp.where(outer, cross_there + term_out, main + term_there)
    pivot, *lates = lax.optimization_barrier((pivot, *lates))
    pivots, panels = ringed(pivot, panel)
    *lates, _ = lax.optimization_barrier((*lates, pivots[0]))
    side = rows_through(False, messages[0], lates)
    side_there = permuted(side, slabs, outwards)
    out = pl.pallas_call(
        second_kernel,
        out_shape=four,
        in_specs=vmem(10),
        out_specs=vmem(1)[0],
        scratch_shapes=[wide] * 4,
        compiler_params=pltpu.CompilerParams(vmem_limit_bytes=VMEM_LIMIT),
        name="second_level",
    )(side, side_there, pivot, *pivots, panel, *panels)
    ends = [permuted(out[step], slabs, to_owner(step)) for step in range(4)]

    def ended(code):
        place_of = lax.rem(line + spot - code + 4, 4)
        result = ends[0]
        for step in range(1, 4):
            result = jnp.where(place_of == step, ends[step], result)
        return result

    final_diag = diag_even[0] + ended(0) + ended(2)
    return final_diag[None], ended(3)[None], ended(1)[None]


def solution(mesh):
    spec = P("slab", None, "orb", None)
    return jax.shard_map(
        shards, mesh=mesh, in_specs=(spec,) * 4, out_specs=(spec,) * 3, check_vma=False
    )
```

```python
import functools

import jax
import jax.numpy as jnp
from jax import lax
from jax.experimental import pallas as pl
from jax.experimental.pallas import tpu as pltpu
from jax.sharding import PartitionSpec as P

SIDE = 4
VMEM_LIMIT = 16 * 1024 * 1024


def permuted(value, slabs, target):
    pairs = []
    for slab in range(slabs):
        for line in range(SIDE):
            for spot in range(SIDE):
                there = target(slab, line, spot)
                if there is None:
                    continue
                to_slab, to_orb = there
                pairs.append((slab * SIDE * SIDE + orb(slab, line, spot), to_slab % slabs * SIDE * SIDE + to_orb))
    return lax.ppermute(value, ("slab", "orb"), pairs)


def orb(slab, line, spot):
    line, spot = line % SIDE, spot % SIDE
    return SIDE * spot + line if slab % 2 == 0 else SIDE * line + spot


def along_spot(step):
    return lambda slab, line, spot: (slab, orb(slab, line, spot + step))


def along_line(step):
    return lambda slab, line, spot: (slab, orb(slab, line + step, spot))


def crossed(slab, line, spot):
    return slab, orb(slab, line, 3 - spot)


def outwards(slab, line, spot):
    return (slab, orb(slab, line, spot - 1)) if spot % 2 else None


def inner(slab, line, spot):
    return (slab, orb(slab, line, spot + 2)) if spot % 2 else None


def to_owner(step):
    def target(slab, line, spot):
        return slab + spot // 2, orb(slab, line, step + spot - line)

    return target


def slab_below(slab, line, spot):
    return slab - 1, orb(slab, line, spot)


def place():
    core = lax.rem(lax.axis_index("slab"), 2)
    index = lax.axis_index("orb")
    y = lax.div(index, SIDE)
    x = lax.rem(index, SIDE)
    return core, jnp.where(core == 0, x, y), jnp.where(core == 0, y, x)


def block_row(core, line, step, block, rows):
    there = lax.rem(line - step + 4, 4)
    index = jnp.where(core == 0, SIDE * block + there, SIDE * there + block)
    return pl.multiple_of(index * rows, rows)


def halves(value):
    high = value.astype(jnp.bfloat16)
    low = (value - high.astype(jnp.float32)).astype(jnp.bfloat16)
    return high, low


def dot(first, second):
    return jnp.dot(first, second, preferred_element_type=jnp.float32)


def product(left_re, left_im, right_high, right_low):
    rows, width = left_re.shape
    high, low = halves(jnp.concatenate([left_re, left_im], 0))
    both = dot(high, right_high) + (dot(high, right_low) + dot(low, right_high))
    return (
        both[:rows, :width] - both[rows:, width:],
        both[:rows, width:] + both[rows:, :width],
    )


def store_block(high_ref, low_ref, row, rows, block_re, block_im):
    width = block_re.shape[1]
    for part, value in enumerate((block_re, block_im)):
        high, low = halves(value)
        columns = slice(part * width, (part + 1) * width)
        high_ref[pl.ds(row, rows), columns] = high
        low_ref[pl.ds(row, rows), columns] = low


def first_kernel(with_diag, *refs):
    messages = refs[0:4]
    below, above, far_green, far_part = refs[4:8]
    greens = (below.at[0], far_green, above.at[0])
    parts = (below.at[1], far_part, above.at[1])
    lefts = refs[8:-6]
    out_ref = refs[-6]
    green_high, green_low, part_high, part_low, left = refs[-5:]
    core, line, spot = place()
    rows = messages[0].shape[2]
    for step in range(4):
        for block in range(4):
            row = block_row(core, line, step, lax.rem(spot - block + 4, 4), rows)
            green = messages[block].at[0] if step == 0 else greens[step - 1].at[block]
            factor = messages[block].at[1] if step == 0 else parts[step - 1].at[block]
            store_block(green_high, green_low, row, rows, green[0], green[1])
            store_block(part_high, part_low, row, rows, factor[0], factor[1])
    for step in range(4):
        own = pl.multiple_of(lax.rem(spot - step + 4, 4) * rows, rows)
        for part in range(2):
            left[part, pl.ds(own, rows), :] = messages[step][2, part] if with_diag else lefts[step][part]
    middle_re, middle_im = product(left[0], left[1], green_high[...], green_low[...])
    outs = product(middle_re, middle_im, part_high[...], part_low[...])
    for part, value in enumerate(outs):
        for block in range(4):
            out_ref[block, part] = -value[block * rows : (block + 1) * rows]
        if with_diag:
            for step in (0, 3):
                block = lax.rem(spot - step + 4, 4)
                diag = messages[step][3, part]
                out_ref[block, part] += jnp.where(lax.rem(spot, 2) == 0, 0.0, diag)


def second_kernel(*refs):
    side_ref, side_there_ref, own, below, above, far_pivot, far_panel = refs[0:7]
    pivots = (own.at[0], below.at[0], far_pivot, above.at[0])
    panels = (own.at[1], below.at[1], far_panel, above.at[1])
    out_ref = refs[7]
    pivot_high, pivot_low, panel_high, panel_low = refs[8:]
    core, line, spot = place()
    rows = side_ref.shape[2]
    width = side_ref.shape[3]
    outer = lax.rem(spot, 2) == 0
    column_iota = lax.broadcasted_iota(jnp.int32, (rows, width), 1)
    row_iota = lax.broadcasted_iota(jnp.int32, (rows, width), 0)
    diag_re = jnp.zeros((1, width), jnp.float32)
    diag_im = jnp.zeros((1, width), jnp.float32)
    for step in range(4):
        for block in range(4):
            row = block_row(core, line, step, block, rows)
            block_re = pivots[step][block, 0]
            block_im = pivots[step][block, 1]
            on_diagonal = column_iota == row_iota + row
            diag_re += jnp.sum(jnp.where(on_diagonal, block_re, 0.0), axis=0, keepdims=True)
            diag_im += jnp.sum(jnp.where(on_diagonal, block_im, 0.0), axis=0, keepdims=True)
            store_block(pivot_high, pivot_low, row, rows, block_re, block_im)
            store_block(panel_high, panel_low, row, rows, panels[step][block, 0], panels[step][block, 1])
    modulus = diag_re * diag_re + diag_im * diag_im
    weight_re = diag_re / modulus
    weight_im = -diag_im / modulus

    def scaled(re, im):
        return re * weight_re - im * weight_im, re * weight_im + im * weight_re

    def times_pivot(re, im):
        return product(re, im, pivot_high[...], pivot_low[...])

    def times_first(re, im):
        re, im = scaled(re, im)
        take_re, take_im = scaled(*times_pivot(re, im))
        return 2.0 * re - take_re, 2.0 * im - take_im

    left_re, left_im = (
        jnp.concatenate([jnp.where(outer, side_there_ref[block, part], side_ref[block, part]) for block in range(4)], 0)
        for part in range(2)
    )
    guess_re, guess_im = times_first(left_re, left_im)
    take_re, take_im = times_first(*times_pivot(guess_re, guess_im))
    solved_re = 2.0 * guess_re - take_re
    solved_im = 2.0 * guess_im - take_im
    outs = product(solved_re, solved_im, panel_high[...], panel_low[...])
    for part, value in enumerate(outs):
        for block in range(4):
            kept = jnp.where(outer, side_ref[block, part], 0.0)
            slot = lax.rem(block + line - spot + 4, 4)
            out_ref[slot, part] = kept - value[block * rows : (block + 1) * rows]


def vmem(count):
    return [pl.BlockSpec(memory_space=pltpu.VMEM)] * count


def shards(diag_even, odd_green, lower, upper):
    rows = lower.shape[2]
    width = lower.shape[3]
    slabs = lax.axis_size("slab")
    core, line, spot = place()
    def message(step):
        there = lax.rem(spot + step, 4)
        odd = lax.div(there, 2)
        green = lax.dynamic_index_in_dim(odd_green, odd, 0, False)
        down = lax.dynamic_index_in_dim(lower, 2 * odd + 1, 0, False)
        up = lax.dynamic_index_in_dim(upper, 2 * odd + 1, 0, False)
        with_lower = (there == 0) | (there == 3)
        blocks = [green, jnp.where(with_lower, down, up), jnp.where(odd == 0, lower[2], upper[2])]
        return jnp.stack(blocks + [diag_even[1]] if step in (0, 3) else blocks)

    def ringed(pair, moved=None):
        below = permuted(pair, slabs, along_line(1))
        above = permuted(pair, slabs, along_line(-1))
        first, second = below[0], above[1]
        if moved is not None:
            moved, _ = lax.optimization_barrier((moved, pair))
            moved = permuted(moved, slabs, slab_below)
            first, _ = lax.optimization_barrier((first, moved))
            second, _ = lax.optimization_barrier((second, moved))
        return moved, (below, above, permuted(first, slabs, along_line(1)), permuted(second, slabs, along_line(-1)))

    messages = [message(0)] + [permuted(message(step), slabs, along_spot(step)) for step in range(1, 4)]
    whole = jnp.stack([jnp.stack([piece[side] for piece in messages]) for side in range(2)])
    next_row, ring = ringed(whole, lower[0])
    four = jax.ShapeDtypeStruct((4, 2, rows, width), jnp.float32)
    wide = pltpu.VMEM((width, 2 * width), jnp.bfloat16)

    def rows_through(with_diag, message, lefts):
        flops = 3 * 2 * 2 * (8 * rows) * width * (2 * width)
        return pl.pallas_call(
            functools.partial(first_kernel, with_diag),
            out_shape=four,
            in_specs=vmem(8 + len(lefts)),
            out_specs=vmem(1)[0],
            scratch_shapes=[wide] * 4 + [pltpu.VMEM((2, 4 * rows, width), jnp.float32)],
            compiler_params=pltpu.CompilerParams(vmem_limit_bytes=VMEM_LIMIT),
            cost_estimate=pl.CostEstimate(flops=flops, bytes_accessed=12 * width * width, transcendentals=0),
            name="first_level" if with_diag else "first_level_side",
        )(message, *messages[1:], *ring, *lefts)

    main = rows_through(True, messages[0], [])

    def late(step):
        return jnp.where(lax.rem(spot + step, 4) < 2, upper[0], next_row)

    lates = [late(0)] + [permuted(late(step), slabs, along_spot(step)) for step in range(1, 4)]

    outer = lax.rem(spot, 2) == 0
    cross_there = permuted(main, slabs, crossed)
    term_out = permuted(main, slabs, outwards)
    term_there = permuted(main, slabs, inner)
    panel = jnp.where(outer, main, cross_there)
    pivot = jnp.where(outer, cross_there + term_out, main + term_there)
    pivot, *lates = lax.optimization_barrier((pivot, *lates))
    pair_own = jnp.stack([pivot, panel])
    _, pairs = ringed(pair_own)
    *lates, _ = lax.optimization_barrier((*lates, pair_own))
    side = rows_through(False, messages[0], lates)
    side_there = permuted(side, slabs, outwards)
    out = pl.pallas_call(
        second_kernel,
        out_shape=four,
        in_specs=vmem(7),
        out_specs=vmem(1)[0],
        scratch_shapes=[wide] * 4,
        compiler_params=pltpu.CompilerParams(vmem_limit_bytes=VMEM_LIMIT),
        name="second_level",
    )(side, side_there, pair_own, *pairs)
    ends = [permuted(out[step], slabs, to_owner(step)) for step in range(4)]

    def ended(code):
        place_of = lax.rem(line + spot - code + 4, 4)
        result = ends[0]
        for step in range(1, 4):
            result = jnp.where(place_of == step, ends[step], result)
        return result

    final_diag = diag_even[0] + ended(0) + ended(2)
    return final_diag[None], ended(3)[None], ended(1)[None]


def solution(mesh):
    spec = P("slab", None, "orb", None)
    return jax.shard_map(
        shards, mesh=mesh, in_specs=(spec,) * 4, out_specs=(spec,) * 3, check_vma=False
    )
```
